32 devices in a mesh: dp: 4 (over x, core), fsdp: 2 (over y), mp: 4 (over z).
Axes of the slice: x: 2, y: 2, z: 4, core: 2. Of those that a mesh axis runs over, the one named last changes fastest.
Arguments:
- inputs: bfloat16 [5120, 1536], P(('dp', 'fsdp', 'mp')), may hold values from -6 to 6
- clip_ids: int32 [5120], P(('dp', 'fsdp')), may hold values from 0 to 3, as said below
- clip_pos: int32 [5120], P(('dp', 'fsdp')), may hold values from 0 to 1535, as said below
- text_states: bfloat16 [4, 64, 1536], replicated, may hold values from -6 to 6
- norm_gain: bfloat16 [2, 3, 1536], P(None, None, 'fsdp'), may hold values from 0.099609375 to 1.8984375
- norm_bias: bfloat16 [2, 3, 1536], P(None, None, 'fsdp'), may hold values from -1.5 to 1.5
- self_qkv: bfloat16 [2, 1536, 3, 1536], P(None, 'fsdp', None, 'mp'), may hold values from -0.15625 to 0.15625
- self_out: bfloat16 [2, 1536, 1536], P(None, 'mp', 'fsdp'), may hold values from -0.625 to 0.625
- cross_q: bfloat16 [2, 1536, 1536], P(None, 'fsdp', 'mp'), may hold values from -0.15625 to 0.15625
- cross_kv: bfloat16 [2, 1536, 2, 1536], P(None, 'fsdp', None, 'mp'), may hold values from -0.15625 to 0.15625
- cross_out: bfloat16 [2, 1536, 1536], P(None, 'mp', 'fsdp'), may hold values from -0.3125 to 0.3125
- mlp_up: bfloat16 [2, 1536, 6144], P(None, 'fsdp', 'mp'), may hold values from -0.15625 to 0.15625
- mlp_down: bfloat16 [2, 6144, 1536], P(None, 'mp', 'fsdp'), may hold values from -0.109375 to 0.109375
- cotangent: bfloat16 [5120, 1536], P(('dp', 'fsdp', 'mp')), may hold values from -6 to 6
Outputs:
- output: bfloat16 [5120, 1536], P(('dp', 'fsdp', 'mp'))
- input_grad: float32 [5120, 1536], P(('dp', 'fsdp', 'mp'))
- text_grad: float32 [4, 64, 1536], replicated
- gain_grad: float32 [2, 3, 1536], P(None, None, 'fsdp')
- bias_grad: float32 [2, 3, 1536], P(None, None, 'fsdp')
- self_qkv_grad: float32 [2, 1536, 3, 1536], P(None, 'fsdp', None, 'mp')
- self_out_grad: float32 [2, 1536, 1536], P(None, 'mp', 'fsdp')
- cross_q_grad: float32 [2, 1536, 1536], P(None, 'fsdp', 'mp')
- cross_kv_grad: float32 [2, 1536, 2, 1536], P(None, 'fsdp', None, 'mp')
- cross_out_grad: float32 [2, 1536, 1536], P(None, 'mp', 'fsdp')
- mlp_up_grad: float32 [2, 1536, 6144], P(None, 'fsdp', 'mp')
- mlp_down_grad: float32 [2, 6144, 1536], P(None, 'mp', 'fsdp')
The draws below stay inside these ranges and needn't reach their ends.
Inputs may be any that keep to these rules, and one draw needn't show every extreme that they name: `clip_ids`: clip numbers never fall along the stream; every clip has 1024 to 1536 frames, one has exactly 1536 and one exactly 1024; clip k's text states are text_states[k]. clip_pos counts from 0 at the first frame of each clip and rises by one a frame within it.
All inputs are finite; a program needn't handle non-finite values.
Results may differ from the reference program's by a relative error of at most 0.03.
Values may be sent and summed in bfloat16 or wider, within the bound.
No kernel may reach another device: no remote copies, remote signals or barrier semaphores. Data moves between devices by JAX's collectives and lax.ppermute only.
A program may use at most 256 MiB of HBM per device.

```python
from functools import partial
import jax
import jax.numpy as jnp
from jax import lax

D = 1536
HEADS = 24
HEAD_DIM = 64
FF = 6144
LAYERS = 2
TEXT = 64
CLIP_LO = 1024
CLIP_HI = 1536
TOK_DEV = 640
TOKENS = 5120
CLIPS = 4
SLOTS = 2
SLOT_LAST = 2
REACH = 3


def clip_layout(key):
    spread = (CLIP_HI - CLIP_LO) // 2
    middle = (CLIP_LO + CLIP_HI) // 2
    half_count = CLIPS // 2
    offsets = jax.random.randint(jax.random.fold_in(key, 11), (half_count,), -spread, spread + 1)
    offsets = offsets.at[0].set(spread)
    lengths = jnp.concatenate([middle + offsets, middle - offsets]).astype(jnp.int32)
    lengths = jax.random.permutation(jax.random.fold_in(key, 12), lengths)
    ends = jnp.cumsum(lengths).astype(jnp.int32)
    starts = ends - lengths
    frames = jnp.arange(TOKENS, dtype=jnp.int32)
    clip_of = jnp.sum((frames[:, None] >= ends[None, :]).astype(jnp.int32), axis=1).astype(jnp.int32)
    position = frames - starts[clip_of]
    return (clip_of, position.astype(jnp.int32))


def draw_clip_ids(key, part):
    return clip_layout(key)[0]


def draw_clip_pos(key, part):
    return clip_layout(key)[1]


def steps_of(stream_key, extent, shards, low, top_value):
    def one(axis_at, blocks):
        heights = jax.random.uniform(jax.random.fold_in(jax.random.fold_in(stream_key, 6), axis_at), (blocks,), jnp.float32, low / len(shards), top_value / len(shards))
        return jnp.repeat(jnp.exp(heights), extent[axis_at] // blocks).reshape((-1,) + (1,) * (len(extent) - axis_at - 1))

    gain = one(*shards[0])
    for cut in shards[1:]:
        gain = gain * one(*cut)
    return gain


def centred(stream_key, extent, scale, most, cuts=(), kind=jnp.bfloat16):
    factor_of = steps_of(stream_key, extent, cuts, -0.22, 0.18) if cuts else 1.0
    values = jax.random.normal(stream_key, extent, jnp.float32) * scale * factor_of
    return jnp.minimum(jnp.maximum(values, -most), most).astype(kind)


def setup_inputs(seed: int = 0) -> dict:
    key_of = jax.random.split(jax.random.key(seed), 15)
    return {
        "inputs": centred(key_of[0], (TOKENS, D), 1.0, 6.0, ((0, 32),)),
        "clip_ids": draw_clip_ids(jax.random.fold_in(key_of[14], 71), 0),
        "clip_pos": draw_clip_pos(jax.random.fold_in(key_of[14], 71), 0),
        "text_states": centred(key_of[3], (CLIPS, TEXT, D), 1.0, 6.0),
        "norm_gain": jnp.clip(1.0 + 0.18 * jax.random.normal(key_of[4], (LAYERS, 3, D), jnp.float32), 0.099609375, 1.8984375).astype(jnp.bfloat16),
        "norm_bias": centred(key_of[5], (LAYERS, 3, D), 0.3, 1.5, ((2, 2),)),
        "self_qkv": centred(key_of[6], (LAYERS, D, 3, D), D ** -0.5, 0.15625, ((1, 2), (3, 4))),
        "self_out": centred(key_of[7], (LAYERS, D, D), (D // 16) ** -0.5, 0.625, ((1, 4), (2, 2))),
        "cross_q": centred(key_of[8], (LAYERS, D, D), D ** -0.5, 0.15625, ((1, 2), (2, 4))),
        "cross_kv": centred(key_of[9], (LAYERS, D, 2, D), D ** -0.5, 0.15625, ((1, 2), (3, 4))),
        "cross_out": centred(key_of[10], (LAYERS, D, D), (D // 4) ** -0.5, 0.3125, ((1, 4), (2, 2))),
        "mlp_up": centred(key_of[11], (LAYERS, D, FF), D ** -0.5, 0.15625, ((1, 2), (2, 4))),
        "mlp_down": centred(key_of[12], (LAYERS, FF, D), (FF // 2) ** -0.5, 0.109375, ((1, 4), (2, 2))),
        "cotangent": centred(key_of[13], (TOKENS, D), 1.0, 6.0, ((0, 32),)),
    }


norm_eps = 1e-05
score_scale = 0.125
masked_fill = -1e+30
highest = lax.Precision.HIGHEST

@jax.custom_vjp
def low(v):
    return lax.optimization_barrier(v.astype(jnp.bfloat16)).astype(jnp.float32)

@jax.custom_vjp
def low_back(v):
    return v

def low_keep(v):
    return (low(v), None)

def low_pass(kept, grad):
    return (grad,)

def back_keep(v):
    return (v, None)

def back_low(kept, grad):
    return (low(grad),)
low.defvjp(low_keep, low_pass)
low_back.defvjp(back_keep, back_low)

def round_both(value):
    return low_back(low(value))

def layer_norm(values, gain_vec, bias_vec):
    center = values - lax.optimization_barrier(jnp.mean(values, axis=-1, keepdims=True))
    spread = lax.optimization_barrier(jnp.mean(center * center, axis=-1, keepdims=True))
    return center * lax.rsqrt(spread + norm_eps) * gain_vec + bias_vec

def self_block(block_index, queries, keys_pad, values_pad, clip_pos):
    first = block_index * TOK_DEV
    width = (REACH + 1) * TOK_DEV
    local_q = lax.dynamic_slice_in_dim(queries, first, TOK_DEV, 0).reshape(TOK_DEV, HEADS, HEAD_DIM)
    local_k = lax.dynamic_slice_in_dim(keys_pad, first, width, 0).reshape(width, HEADS, HEAD_DIM)
    local_v = lax.dynamic_slice_in_dim(values_pad, first, width, 0).reshape(width, HEADS, HEAD_DIM)
    query_pos = first + jnp.arange(TOK_DEV, dtype=jnp.int32)
    key_pos = first - REACH * TOK_DEV + jnp.arange(width, dtype=jnp.int32)
    starts = query_pos - lax.dynamic_slice_in_dim(clip_pos, first, TOK_DEV, 0)
    allowed = (key_pos[None, :] <= query_pos[:, None]) & (key_pos[None, :] >= starts[:, None])
    scores = low_back(jnp.einsum('qhe,khe->hqk', local_q, local_k, precision=highest) * score_scale)
    scores = jnp.where(allowed[None], scores, masked_fill)
    probs = low(jax.nn.softmax(scores, axis=-1))
    return jnp.einsum('hqk,khe->qhe', probs, local_v, precision=highest).reshape(TOK_DEV, D)

def cross_block(block_index, cross_queries, text_flat, kv_weight, clip_ids):
    first = block_index * TOK_DEV
    ids_here = lax.dynamic_slice_in_dim(clip_ids, first, TOK_DEV, 0)
    slot_first = jnp.minimum(ids_here[0], SLOT_LAST).astype(jnp.int32)
    picked = lax.dynamic_slice_in_dim(text_flat, slot_first * TEXT, SLOTS * TEXT, 0)
    text_kv = round_both(jnp.einsum('sd,dcj->csj', picked, kv_weight, precision=highest))
    slot_ids = slot_first + jnp.arange(SLOTS * TEXT, dtype=jnp.int32) // TEXT
    allowed = ids_here[:, None] == slot_ids[None, :]
    local_q = lax.dynamic_slice_in_dim(cross_queries, first, TOK_DEV, 0).reshape(TOK_DEV, HEADS, HEAD_DIM)
    text_k = text_kv[0].reshape(SLOTS * TEXT, HEADS, HEAD_DIM)
    text_v = text_kv[1].reshape(SLOTS * TEXT, HEADS, HEAD_DIM)
    scores = low_back(jnp.einsum('qhe,khe->hqk', local_q, text_k, precision=highest) * score_scale)
    scores = jnp.where(allowed[None], scores, masked_fill)
    probs = low(jax.nn.softmax(scores, axis=-1))
    return jnp.einsum('hqk,khe->qhe', probs, text_v, precision=highest).reshape(TOK_DEV, D)

def forward(inputs, text_states, norm_gain, norm_bias, self_qkv, self_out, cross_q, cross_kv, cross_out, mlp_up, mlp_down, clip_ids, clip_pos):
    tokens = inputs.shape[0]
    blocks = tokens // TOK_DEV
    block_list = jnp.arange(blocks, dtype=jnp.int32)
    padding = jnp.zeros((REACH * TOK_DEV, D), jnp.float32)
    text_flat = text_states.reshape(CLIPS * TEXT, D)
    hidden = inputs
    for layer_index in range(LAYERS):
        normed = low(layer_norm(hidden, norm_gain[layer_index, 0], norm_bias[layer_index, 0]))
        projected = jnp.einsum('td,dcj->ctj', normed, self_qkv[layer_index], precision=highest)
        queries = round_both(projected[0])
        keys_pad = jnp.concatenate([padding, round_both(projected[1])], axis=0)
        values_pad = jnp.concatenate([padding, round_both(projected[2])], axis=0)
        attended = lax.map(jax.checkpoint(lambda block_index: self_block(block_index, queries, keys_pad, values_pad, clip_pos)), block_list)
        attended = round_both(attended.reshape(tokens, D))
        hidden = hidden + low_back(jnp.dot(attended, self_out[layer_index], precision=highest))
        normed = low(layer_norm(hidden, norm_gain[layer_index, 1], norm_bias[layer_index, 1]))
        cross_queries = round_both(jnp.dot(normed, cross_q[layer_index], precision=highest))
        kv_weight = cross_kv[layer_index]
        crossed = lax.map(jax.checkpoint(lambda block_index: cross_block(block_index, cross_queries, text_flat, kv_weight, clip_ids)), block_list)
        crossed = round_both(crossed.reshape(tokens, D))
        hidden = hidden + low_back(jnp.dot(crossed, cross_out[layer_index], precision=highest))
        normed = low(layer_norm(hidden, norm_gain[layer_index, 2], norm_bias[layer_index, 2]))
        upward = low_back(jnp.dot(normed, mlp_up[layer_index], precision=highest))
        activated = low(jax.nn.gelu(upward))
        hidden = hidden + low_back(jnp.dot(activated, mlp_down[layer_index], precision=highest))
    return hidden

def reference(inputs, clip_ids, clip_pos, text_states, norm_gain, norm_bias, self_qkv, self_out, cross_q, cross_kv, cross_out, mlp_up, mlp_down, cotangent):
    floats = [array_in.astype(jnp.float32) for array_in in (inputs, text_states, norm_gain, norm_bias, self_qkv, self_out, cross_q, cross_kv, cross_out, mlp_up, mlp_down)]
    result, pull = jax.vjp(partial(forward, clip_ids=clip_ids, clip_pos=clip_pos), *floats)
    grads = pull(cotangent.astype(jnp.float32))
    return (result.astype(jnp.bfloat16), grads[0], grads[1], grads[2], grads[3], grads[4], grads[5], grads[6], grads[7], grads[8], grads[9], grads[10])
```

```python
import functools

import jax
import jax.numpy as jnp
from jax import lax
from jax.experimental import pallas as pl
from jax.experimental.pallas import tpu as pltpu
from jax.sharding import PartitionSpec as P

HEAD_DIM = 64
TEXT = 64
SLOTS = 2
REACH = 3
CLIP_HI = 1536
LANES = 128

norm_eps = 1e-05
score_scale = 0.125
masked_fill = -1e30
gelu_root = 0.7978845608028654
gelu_cubic = 0.044715
bf16 = jnp.bfloat16
f32 = jnp.float32
NT = (((1,), (1,)), ((), ()))
NN = (((1,), (0,)), ((), ()))
TN = (((0,), (0,)), ((), ()))


def mm(a, b, dims=NN):
    return lax.dot_general(a, b, dims, preferred_element_type=f32)


def passed_along(value, axis, steps):
    count = lax.axis_size(axis)
    leading, last = (max(0, -steps), min(count, count - steps))
    return lax.ppermute(value, axis, [(source, source + steps) for source in range(leading, last)])


def swapped(value, axis, mask):
    count = lax.axis_size(axis)
    return lax.ppermute(value, axis, [(source, source ^ mask) for source in range(count)])


def ordered(bit, own, other, axis):
    lower = jnp.where(bit == 0, own, other)
    upper = jnp.where(bit == 0, other, own)
    return jnp.concatenate([lower, upper], axis=axis)


def part_of(value, index, size, axis):
    return lax.dynamic_slice_in_dim(value, index * size, size, axis)


def stack_heads(block):
    lane = lax.broadcasted_iota(jnp.int32, block.shape, 1)
    zero = jnp.zeros_like(block)
    return jnp.concatenate(
        [jnp.where(lane < HEAD_DIM, block, zero), jnp.where(lane < HEAD_DIM, zero, block)], axis=0
    )


def unstack_heads(block):
    rows = block.shape[0] // 2
    lane = lax.broadcasted_iota(jnp.int32, (rows, block.shape[1]), 1)
    return jnp.where(lane < HEAD_DIM, block[:rows], block[rows:])


def self_forward_kernel(sizes, cs_ref, q_ref, k0, v0, k1, v1, k2, v2, k3, v3, o_ref, lse_ref):
    tok, tail = sizes
    spans = [(k3, v3, 0, tail), (k2, v2, tail, tok), (k1, v1, tail + tok, tok), (k0, v0, tail + 2 * tok, tok)]
    span = tail + 2 * tok
    rows = LANES
    for step in range(tok // rows):
        first = step * rows
        low, high = first, first + span + rows
        queries = stack_heads(q_ref[first : first + rows, :] * bf16(score_scale))
        starts = cs_ref[first : first + rows, :]
        starts = jnp.concatenate([starts, starts], axis=0)
        parts = []
        for key_ref, value_ref, base, length in spans:
            begin, end = max(low, base), min(high, base + length)
            if begin >= end:
                continue
            keys = key_ref[begin - base : end - base, :]
            scores = mm(queries, keys, NT)
            column = lax.broadcasted_iota(jnp.int32, scores.shape, 1) + begin
            allowed = column >= starts
            if base + length > span:
                row = lax.broadcasted_iota(jnp.int32, scores.shape, 0)
                row = jnp.where(row >= rows, row - rows, row) + (first + span)
                allowed = allowed & (column <= row)
            scores = jnp.where(allowed, scores, masked_fill)
            parts.append((scores, value_ref, begin - base, end - base))
        top = functools.reduce(
            jnp.maximum, [jnp.max(part[0], axis=1, keepdims=True) for part in parts]
        )
        total = jnp.zeros_like(top)
        acc = jnp.zeros((2 * rows, LANES), f32)
        for scores, value_ref, begin, end in parts:
            expanded = jnp.exp(scores - top)
            total = total + jnp.sum(expanded, axis=1, keepdims=True)
            acc = acc + mm(expanded.astype(bf16), value_ref[begin:end, :])
        o_ref[first : first + rows, :] = unstack_heads(acc / total).astype(bf16)
        log_total = top + jnp.log(total)
        lse_ref[first : first + rows, :] = jnp.concatenate(
            [log_total[:rows], log_total[rows:]], axis=1
        )


def self_forward(projected, pieces, starts_col):
    tok, width = projected.shape[1:]
    tail = pieces[2].shape[1]
    pairs = width // LANES

    def spec(part, length):
        return pl.BlockSpec((None, length, LANES), lambda pair, part=part: (part, 0, pair))

    in_specs = [pl.BlockSpec((tok, 1), lambda pair: (0, 0)), spec(0, tok), spec(1, tok), spec(2, tok)]
    operands = [starts_col, projected, projected, projected]
    for piece in pieces:
        in_specs += [spec(0, piece.shape[1]), spec(1, piece.shape[1])]
        operands += [piece, piece]
    area = tok * (tail + 2 * tok + LANES)
    return pl.pallas_call(
        functools.partial(self_forward_kernel, (tok, tail)),
        grid=(pairs,),
        in_specs=in_specs,
        out_specs=[
            pl.BlockSpec((tok, LANES), lambda pair: (0, pair)),
            pl.BlockSpec((None, tok, 2), lambda pair: (pair, 0, 0)),
        ],
        out_shape=[
            jax.ShapeDtypeStruct((tok, width), bf16),
            jax.ShapeDtypeStruct((pairs, tok, 2), f32),
        ],
        compiler_params=pltpu.CompilerParams(vmem_limit_bytes=48 * 1024 * 1024),
        cost_estimate=pl.CostEstimate(
            flops=4 * area * width, bytes_accessed=8 * tok * width * 2, transcendentals=area * 2 * pairs
        ),
        name="self_attention",
    )(*operands)


def self_backward_kernel(
    sizes, cs_ref, lse_ref, delta_ref, q_ref, do_ref, k0, v0, k1, v1, k2, v2, k3, v3,
    dq_ref, d0, d1, d2, d3, dq_acc, q_st, do_st,
):
    tok, tail = sizes
    half = tok // 2
    span = tail + 2 * tok
    lane = lax.broadcasted_iota(jnp.int32, (tok, LANES), 1)
    queries = q_ref[...] * bf16(score_scale)
    grads = do_ref[...]
    zero = jnp.zeros_like(queries)
    q_st[0] = jnp.where(lane < HEAD_DIM, queries, zero)
    q_st[1] = jnp.where(lane < HEAD_DIM, zero, queries)
    do_st[0] = jnp.where(lane < HEAD_DIM, grads, zero)
    do_st[1] = jnp.where(lane < HEAD_DIM, zero, grads)
    dq_acc[...] = jnp.zeros_like(dq_acc)
    blocks = [(k3, v3, d3, 0, 0, tail)]
    for key_ref, value_ref, out_ref, base in ((k2, v2, d2, tail), (k1, v1, d1, tail + tok), (k0, v0, d0, span)):
        blocks += [(key_ref, value_ref, out_ref, base, 0, half), (key_ref, value_ref, out_ref, base, half, half)]
    for key_ref, value_ref, out_ref, base, offset, length in blocks:
        first = base + offset
        q_low = max(0, first - span)
        q_high = min(tok, -(-(first + length) // LANES) * LANES)
        keys = key_ref[offset : offset + length, :]
        values = value_ref[offset : offset + length, :]
        grad_keys = jnp.zeros((length, LANES), f32)
        grad_values = jnp.zeros((length, LANES), f32)
        for head in range(2):
            queries = q_st[head, q_low:q_high, :]
            grads = do_st[head, q_low:q_high, :]
            scores = mm(keys, queries, NT)
            row = lax.broadcasted_iota(jnp.int32, scores.shape, 0) + first
            allowed = row >= cs_ref[:, q_low:q_high]
            if base == span:
                column = lax.broadcasted_iota(jnp.int32, scores.shape, 1) + (q_low + span)
                allowed = allowed & (row <= column)
            probs = jnp.where(allowed, jnp.exp(scores - lse_ref[head : head + 1, q_low:q_high]), 0.0)
            grad_probs = mm(values, grads, NT)
            grad_scores = (probs * (grad_probs - delta_ref[head : head + 1, q_low:q_high])).astype(bf16)
            grad_values = grad_values + mm(probs.astype(bf16), grads)
            grad_keys = grad_keys + mm(grad_scores, queries)
            dq_acc[head, q_low:q_high, :] += mm(grad_scores, keys, TN)
        out_ref[0, offset : offset + length, :] = grad_keys.astype(out_ref.dtype)
        out_ref[1, offset : offset + length, :] = grad_values.astype(out_ref.dtype)
    dq_ref[...] = (jnp.where(lane < HEAD_DIM, dq_acc[0], dq_acc[1]) * score_scale).astype(bf16)


def self_backward(projected, pieces, starts_row, log_total, delta, grad_out):
    tok, width = projected.shape[1:]
    tail = pieces[2].shape[1]
    pairs = width // LANES

    def spec(part, length):
        return pl.BlockSpec((None, length, LANES), lambda pair, part=part: (part, 0, pair))

    def both(length):
        return pl.BlockSpec((2, length, LANES), lambda pair: (0, 0, pair))

    flat = pl.BlockSpec((tok, LANES), lambda pair: (0, pair))
    stat = pl.BlockSpec((None, 2, tok), lambda pair: (pair, 0, 0))
    in_specs = [pl.BlockSpec((1, tok), lambda pair: (0, 0)), stat, stat, spec(0, tok), flat, spec(1, tok), spec(2, tok)]
    operands = [starts_row, log_total, delta, projected, grad_out, projected, projected]
    out_specs = [flat, both(tok)]
    out_shape = [jax.ShapeDtypeStruct((tok, width), bf16), jax.ShapeDtypeStruct((2, tok, width), f32)]
    for piece in pieces:
        in_specs += [spec(0, piece.shape[1]), spec(1, piece.shape[1])]
        operands += [piece, piece]
        out_specs.append(both(piece.shape[1]))
        out_shape.append(jax.ShapeDtypeStruct(piece.shape, bf16))
    area = tok * (tail + 2 * tok + LANES)
    return pl.pallas_call(
        functools.partial(self_backward_kernel, (tok, tail)),
        grid=(pairs,),
        in_specs=in_specs,
        out_specs=out_specs,
        out_shape=out_shape,
        scratch_shapes=[
            pltpu.VMEM((2, tok, LANES), f32),
            pltpu.VMEM((2, tok, LANES), bf16),
            pltpu.VMEM((2, tok, LANES), bf16),
        ],
        compiler_params=pltpu.CompilerParams(vmem_limit_bytes=48 * 1024 * 1024),
        cost_estimate=pl.CostEstimate(
            flops=10 * area * width, bytes_accessed=16 * tok * width * 2, transcendentals=area * 2 * pairs
        ),
        name="self_attention_back",
    )(*operands)


def cross_forward_kernel(ids_ref, slot_ref, q_ref, k_ref, v_ref, o_ref):
    allowed = ids_ref[...] == slot_ref[...]
    for pair in range(q_ref.shape[1] // LANES):
        cols = slice(pair * LANES, (pair + 1) * LANES)
        queries = stack_heads(q_ref[:, cols] * bf16(score_scale))
        scores = mm(queries, k_ref[:, cols], NT)
        rows = scores.shape[0] // 2
        halves = []
        for head in range(2):
            part = jnp.where(allowed, scores[head * rows : (head + 1) * rows], masked_fill)
            expanded = jnp.exp(part - jnp.max(part, axis=1, keepdims=True))
            halves.append(expanded / jnp.sum(expanded, axis=1, keepdims=True))
        probs = jnp.concatenate(halves, axis=0).astype(bf16)
        o_ref[:, cols] = unstack_heads(mm(probs, v_ref[:, cols])).astype(bf16)


def cross_backward_kernel(ids_ref, slot_ref, q_ref, do_ref, k_ref, v_ref, dq_ref, dk_ref, dv_ref):
    allowed = ids_ref[...] == slot_ref[...]
    for pair in range(q_ref.shape[1] // LANES):
        cols = slice(pair * LANES, (pair + 1) * LANES)
        queries = stack_heads(q_ref[:, cols] * bf16(score_scale))
        grads = stack_heads(do_ref[:, cols])
        keys = k_ref[:, cols]
        scores = mm(queries, keys, NT)
        grad_probs = mm(grads, v_ref[:, cols], NT)
        rows = scores.shape[0] // 2
        probs, grad_scores = [], []
        for head in range(2):
            part = jnp.where(allowed, scores[head * rows : (head + 1) * rows], masked_fill)
            expanded = jnp.exp(part - jnp.max(part, axis=1, keepdims=True))
            prob = expanded / jnp.sum(expanded, axis=1, keepdims=True)
            back = grad_probs[head * rows : (head + 1) * rows]
            inner = jnp.sum(prob * back, axis=1, keepdims=True)
            probs.append(prob.astype(bf16))
            grad_scores.append((prob * (back - inner)).astype(bf16))
        probs = jnp.concatenate(probs, axis=0)
        grad_scores = jnp.concatenate(grad_scores, axis=0)
        dq_ref[:, cols] = unstack_heads(mm(grad_scores, keys) * score_scale).astype(bf16)
        dk_ref[:, cols] = mm(grad_scores, queries, TN).astype(dk_ref.dtype)
        dv_ref[:, cols] = mm(probs, grads, TN).astype(dv_ref.dtype)


def cross_call(kernel, outs, ids_col, slot_row, rows, text):
    count, width = rows[0].shape
    keys = text[0].shape[0]
    chunk = width // 3 if width % (3 * LANES) == 0 else width
    row_spec = pl.BlockSpec((count, chunk), lambda group: (0, group))
    text_spec = pl.BlockSpec((keys, chunk), lambda group: (0, group))
    return pl.pallas_call(
        kernel,
        grid=(width // chunk,),
        in_specs=[
            pl.BlockSpec((count, 1), lambda group: (0, 0)),
            pl.BlockSpec((1, keys), lambda group: (0, 0)),
        ]
        + [row_spec] * len(rows)
        + [text_spec] * len(text),
        out_specs=[row_spec if shape.shape[0] == count else text_spec for shape in outs],
        out_shape=outs,
        cost_estimate=pl.CostEstimate(
            flops=4 * len(outs) * count * keys * width,
            bytes_accessed=2 * width * (count + keys) * 3,
            transcendentals=count * keys * width // HEAD_DIM,
        ),
        name="cross_attention" if len(outs) == 1 else "cross_attention_back",
    )(ids_col, slot_row, *rows, *text)


def layer_norm(values, gain_vec, bias_vec):
    center = values - jnp.mean(values, axis=-1, keepdims=True)
    spread = jnp.mean(center * center, axis=-1, keepdims=True)
    return center * lax.rsqrt(spread + norm_eps) * gain_vec + bias_vec


def layer_norm_back(values, gain_vec, grad):
    center = values - jnp.mean(values, axis=-1, keepdims=True)
    spread = jnp.mean(center * center, axis=-1, keepdims=True)
    scale = lax.rsqrt(spread + norm_eps)
    unit = center * scale
    inner = grad * gain_vec
    mean_inner = jnp.mean(inner, axis=-1, keepdims=True)
    mean_cross = jnp.mean(inner * unit, axis=-1, keepdims=True)
    result = scale * (inner - mean_inner - unit * mean_cross)
    return (result, jnp.sum(grad * unit, axis=0), jnp.sum(grad, axis=0))


def local(
    inputs, clip_ids, clip_pos, text_states, norm_gain, norm_bias, self_qkv, self_out,
    cross_q, cross_kv, cross_out, mlp_up, mlp_down, cotangent,
):
    tok_count = clip_ids.shape[0]
    layer_count = norm_gain.shape[0]
    clip_count = text_states.shape[0]
    own_count, model_width = inputs.shape
    dp_count, fs_count, mp_count = (lax.axis_size(name) for name in ("dp", "fsdp", "mp"))
    pairwise = dp_count == 4
    paired = pairwise and fs_count == 2
    dp_index, fs_index, mp_index = (lax.axis_index(name) for name in ("dp", "fsdp", "mp"))
    core, cross_x = dp_index % 2, dp_index // 2
    cell = model_width // 4
    slice_width = self_out.shape[1]
    half_slice = slice_width // 2

    if paired:
        cells = [
            2 * fs_index + core, 2 * (1 - fs_index) + core,
            2 * fs_index + 1 - core, 2 * (1 - fs_index) + 1 - core,
        ]
        places = [
            jnp.where(number // 2 == fs_index, 0, 1) + 2 * jnp.where(number % 2 == core, 0, 1)
            for number in range(4)
        ]

    def pick_cells(values, order):
        if not paired:
            return values
        axis = values.ndim - 1
        return jnp.concatenate([part_of(values, place, cell, axis) for place in order], axis=axis)

    def to_local(values):
        return pick_cells(values, cells if paired else None)

    def to_global(values):
        return pick_cells(values, places if paired else None)

    def spread_rows(values):
        return lax.all_gather(values, "mp", axis=0, tiled=True)

    def reduce_rows(values):
        return lax.psum_scatter(
            values.astype(bf16), "mp", scatter_dimension=0, tiled=True
        ).astype(f32)

    def gather_slice(shard, axis):
        if not paired:
            return lax.all_gather(shard, "fsdp", axis=axis, tiled=True)
        own = part_of(shard, core, cell, axis)
        far = swapped(own, "fsdp", 1)
        return jnp.concatenate(
            [own, far, part_of(shard, 1 - core, cell, axis), swapped(far, "dp", 1)], axis=axis
        )

    def gather_square(shard, axis):
        heads = 1 - axis
        if not paired:
            whole = lax.all_gather(shard, "fsdp", axis=axis, tiled=True)
            return lax.all_gather(whole, "mp", axis=heads, tiled=True)
        part = part_of(part_of(shard, core, cell, axis), cross_x, half_slice, heads)
        part = lax.all_gather(part, "mp", axis=0, tiled=False)
        part = jnp.concatenate([part, swapped(part, "fsdp", 1)], axis=axis + 1)
        part = jnp.expand_dims(part, heads + 1)
        part = ordered(cross_x, part, swapped(part, "dp", 2), heads + 1)
        if heads == 0:
            part = part.reshape(mp_count * slice_width, 2 * cell)
        else:
            part = part.reshape(mp_count, 2 * cell, slice_width)
            part = part.transpose(1, 0, 2).reshape(2 * cell, mp_count * slice_width)
        return jnp.concatenate([part, swapped(part, "dp", 1)], axis=axis)

    def sum_narrow(own, other):
        return (own.astype(f32) + other.astype(f32)).astype(bf16)

    def reduce_over_replicas(value, axis):
        value = value.astype(bf16)
        if paired:
            keep = lax.slice_in_dim(value, 0, 2 * cell, axis=axis)
            value = sum_narrow(keep, swapped(lax.slice_in_dim(value, 2 * cell, 4 * cell, axis=axis), "dp", 1))
            keep = lax.slice_in_dim(value, 0, cell, axis=axis)
            return sum_narrow(keep, swapped(lax.slice_in_dim(value, cell, 2 * cell, axis=axis), "fsdp", 1))
        return lax.psum_scatter(value, "fsdp", scatter_dimension=axis, tiled=True)

    def reduce_slice(value, axis):
        value = reduce_over_replicas(value, axis)
        if not paired:
            return lax.psum(value, "dp").astype(f32)
        value = sum_narrow(value, swapped(value, "dp", 2))
        return ordered(core, value, swapped(value, "dp", 1), axis).astype(f32)

    def reduce_square(value, axis):
        heads = 1 - axis
        if not paired:
            value = reduce_over_replicas(value, axis)
            value = lax.psum_scatter(value, "mp", scatter_dimension=heads, tiled=True)
            return lax.psum(value, "dp").astype(f32)
        value = reduce_over_replicas(value, axis)
        shape = value.shape[:heads] + (mp_count, 2, half_slice) + value.shape[heads + 1 :]
        value = value.reshape(shape)
        sent = swapped(part_of(value, 1 - cross_x, 1, heads + 1), "dp", 2)
        value = sum_narrow(part_of(value, cross_x, 1, heads + 1), sent)
        value = lax.psum_scatter(value, "mp", scatter_dimension=heads, tiled=True)
        value = jnp.squeeze(value, (heads, heads + 1))
        value = ordered(cross_x, value, swapped(value, "dp", 2), heads)
        return ordered(core, value, swapped(value, "dp", 1), axis).astype(f32)

    def sum_everywhere(value, axes):
        for axis in axes:
            count = lax.axis_size(axis)
            if count in (2, 4):
                mask = 1
                while mask < count:
                    value = value + swapped(value, axis, mask)
                    mask *= 2
            else:
                value = lax.psum(value, axis)
        return value

    group_base = lax.axis_index(("dp", "fsdp")) * tok_count
    tail = CLIP_HI - 2 * tok_count
    clip_start = (
        jnp.arange(tok_count, dtype=jnp.int32) + (tail + 2 * tok_count) - clip_pos
    )
    starts_col, starts_row = clip_start[:, None], clip_start[None, :]
    slot_first = jnp.minimum(clip_ids[0], clip_count - SLOTS)
    slot_row = (slot_first + jnp.arange(SLOTS * TEXT, dtype=jnp.int32) // TEXT)[None, :]
    ids_col = part_of(clip_ids, mp_index, own_count, 0)[:, None]
    text_rows = to_local(
        lax.dynamic_slice_in_dim(text_states, slot_first, SLOTS, 0).reshape(SLOTS * TEXT, model_width)
    )
    norms = jnp.concatenate([norm_gain, norm_bias], axis=1)
    norms = to_local(lax.all_gather(norms, "fsdp", axis=2, tiled=True)).astype(f32)
    gains, biases = norms[:, :3], norms[:, 3:]

    residual = to_local(inputs).astype(f32)
    saved = []
    for layer in range(layer_count):
        w_qkv = gather_slice(self_qkv[layer], 0)
        w_kv = gather_slice(cross_kv[layer], 0)
        w_so = gather_square(self_out[layer], 1)
        w_cq = gather_square(cross_q[layer], 0)
        w_co = gather_square(cross_out[layer], 1)
        w_up = gather_slice(mlp_up[layer], 0)
        w_down = gather_slice(mlp_down[layer], 1)

        start_res = residual
        normed = layer_norm(residual, gains[layer, 0], biases[layer, 0]).astype(bf16)
        rows_one = spread_rows(normed)
        projected = jnp.einsum("td,dcj->ctj", rows_one, w_qkv, preferred_element_type=f32).astype(bf16)
        key_values = projected[1:]
        pieces = [
            passed_along(key_values, ("dp", "fsdp"), 1),
            passed_along(key_values, ("dp", "fsdp"), 2),
            passed_along(key_values[:, tok_count - tail :], ("dp", "fsdp"), 3),
        ]
        heads_out, log_self = self_forward(projected, pieces, starts_col)
        merged_one = lax.all_to_all(heads_out, "mp", split_axis=0, concat_axis=1, tiled=True)
        residual = residual + mm(merged_one, w_so)
        mid_res = residual
        normed_two = layer_norm(residual, gains[layer, 1], biases[layer, 1]).astype(bf16)
        cross_query = mm(normed_two, w_cq).astype(bf16)
        text_kv = jnp.einsum("sd,dcj->csj", text_rows, w_kv, preferred_element_type=f32).astype(bf16)
        text_kv = lax.all_gather(text_kv, "mp", axis=2, tiled=True)
        text_k, text_v = text_kv[0], text_kv[1]
        (merged_two,) = cross_call(
            cross_forward_kernel,
            [jax.ShapeDtypeStruct((own_count, model_width), bf16)],
            ids_col, slot_row, [cross_query], [text_k, text_v],
        )
        residual = residual + mm(merged_two, w_co)
        late_res = residual
        normed = layer_norm(residual, gains[layer, 2], biases[layer, 2]).astype(bf16)
        rows_three = spread_rows(normed)
        upward = mm(rows_three, w_up)
        activated = jax.nn.gelu(upward).astype(bf16)
        residual = residual + reduce_rows(mm(activated, w_down))
        saved.append(
            (
                (w_qkv, w_kv, w_so, w_cq, w_co, w_up, w_down),
                start_res, mid_res, late_res, rows_one, projected, pieces, heads_out, log_self,
                merged_one, normed_two, cross_query, text_k, text_v, merged_two, rows_three,
                upward, activated,
            )
        )
    output = to_global(residual.astype(bf16))

    grad_res = to_local(cotangent).astype(f32)
    text_acc = jnp.zeros((SLOTS * TEXT, model_width), f32)
    matrix_list, gain_list, bias_list = [], [], []
    for layer in reversed(range(layer_count)):
        (
            (w_qkv, w_kv, w_so, w_cq, w_co, w_up, w_down),
            start_res, mid_res, late_res, rows_one, projected, pieces, heads_out, log_self,
            merged_one, normed_two, cross_query, text_k, text_v, merged_two, rows_three,
            upward, activated,
        ) = saved[layer]
        grad_full = spread_rows(grad_res.astype(bf16))
        grad_act = mm(grad_full, w_down, NT)
        grad_up_rows = jax.vjp(jax.nn.gelu, upward)[1](grad_act)[0].astype(bf16)
        grad_normed = reduce_rows(mm(grad_up_rows, w_up, NT))
        grad_down = reduce_slice(mm(activated, grad_full, TN), 1)
        grad_up = reduce_slice(mm(rows_three, grad_up_rows, TN), 0)
        res_part, gain_three, bias_three = layer_norm_back(late_res, gains[layer, 2], grad_normed)
        grad_res = grad_res + res_part
        narrow = grad_res.astype(bf16)
        grad_merged = mm(narrow, w_co, NT).astype(bf16)
        grad_cq_rows, grad_tk, grad_tv = cross_call(
            cross_backward_kernel,
            [
                jax.ShapeDtypeStruct((own_count, model_width), bf16),
                jax.ShapeDtypeStruct((SLOTS * TEXT, model_width), bf16),
                jax.ShapeDtypeStruct((SLOTS * TEXT, model_width), bf16),
            ],
            ids_col, slot_row, [cross_query, grad_merged], [text_k, text_v],
        )
        grad_co = reduce_square(mm(merged_two, narrow, TN), 1)
        grad_cq = reduce_square(mm(normed_two, grad_cq_rows, TN), 0)
        grad_normed = mm(grad_cq_rows, w_cq, NT)
        res_part, gain_two, bias_two = layer_norm_back(mid_res, gains[layer, 1], grad_normed)
        grad_res = grad_res + res_part
        narrow = grad_res.astype(bf16)
        grad_merged = mm(narrow, w_so, NT).astype(bf16)
        grad_heads = lax.all_to_all(grad_merged, "mp", split_axis=1, concat_axis=0, tiled=True)
        grad_so = reduce_square(mm(merged_one, narrow, TN), 1)
        grad_text_kv = lax.psum_scatter(
            jnp.stack([grad_tk, grad_tv]), "mp", scatter_dimension=2, tiled=True
        )
        grad_kv = reduce_slice(
            jnp.einsum("sd,csj->dcj", text_rows, grad_text_kv, preferred_element_type=f32), 0
        )
        text_acc = text_acc + jnp.einsum(
            "csj,dcj->sd", grad_text_kv, w_kv, preferred_element_type=f32
        )
        pairs = heads_out.shape[1] // LANES
        delta = (grad_heads.astype(f32) * heads_out.astype(f32)).reshape(tok_count, 2 * pairs, HEAD_DIM)
        delta = jnp.sum(delta, axis=2).T.reshape(pairs, 2, tok_count)
        grad_q, own_kv, *far_kv = self_backward(
            projected, pieces, starts_row, log_self.transpose(0, 2, 1), delta, grad_heads
        )
        own_kv = own_kv + passed_along(far_kv[0], ("dp", "fsdp"), -1).astype(f32)
        own_kv = own_kv + passed_along(far_kv[1], ("dp", "fsdp"), -2).astype(f32)
        far_tail = passed_along(far_kv[2], ("dp", "fsdp"), -3).astype(f32)
        own_kv = own_kv + jnp.pad(far_tail, ((0, 0), (tok_count - tail, 0), (0, 0)))
        grad_proj = jnp.concatenate([grad_q[None], own_kv.astype(bf16)], axis=0)
        grad_normed = reduce_rows(
            jnp.einsum("ctj,dcj->td", grad_proj, w_qkv, preferred_element_type=f32)
        )
        grad_qkv = reduce_slice(
            jnp.einsum("td,ctj->dcj", rows_one, grad_proj, preferred_element_type=f32), 0
        )
        res_part, gain_one, bias_one = layer_norm_back(start_res, gains[layer, 0], grad_normed)
        grad_res = grad_res + res_part
        gain_list.insert(0, jnp.stack([gain_one, gain_two, gain_three]))
        bias_list.insert(0, jnp.stack([bias_one, bias_two, bias_three]))
        matrix_list.insert(0, (grad_qkv, grad_so, grad_cq, grad_kv, grad_co, grad_up, grad_down))

    stacked = [jnp.stack([layer_set[member] for layer_set in matrix_list]) for member in range(7)]
    norm_grads = to_global(jnp.stack([jnp.stack(gain_list), jnp.stack(bias_list)]))
    norm_grads = sum_everywhere(norm_grads, ("mp", "dp", "fsdp"))
    norm_grads = part_of(norm_grads, fs_index, model_width // fs_count, 3)

    text_full = jnp.zeros((clip_count, TEXT, model_width), f32)
    text_full = lax.dynamic_update_slice_in_dim(
        text_full, to_global(text_acc).reshape(SLOTS, TEXT, model_width), slot_first, 0
    )
    text_grad = lax.psum(text_full, ("dp", "fsdp", "mp"))
    return (output, to_global(grad_res), text_grad, norm_grads[0], norm_grads[1], *stacked)


def solution(mesh):
    in_specs = (
        P(("dp", "fsdp", "mp"), None),
        P(("dp", "fsdp")),
        P(("dp", "fsdp")),
        P(),
        P(None, None, "fsdp"),
        P(None, None, "fsdp"),
        P(None, "fsdp", None, "mp"),
        P(None, "mp", "fsdp"),
        P(None, "fsdp", "mp"),
        P(None, "fsdp", None, "mp"),
        P(None, "mp", "fsdp"),
        P(None, "fsdp", "mp"),
        P(None, "mp", "fsdp"),
        P(("dp", "fsdp", "mp"), None),
    )
    out_specs = (
        P(("dp", "fsdp", "mp"), None),
        P(("dp", "fsdp", "mp"), None),
        P(),
        P(None, None, "fsdp"),
        P(None, None, "fsdp"),
        P(None, "fsdp", None, "mp"),
        P(None, "mp", "fsdp"),
        P(None, "fsdp", "mp"),
        P(None, "fsdp", None, "mp"),
        P(None, "mp", "fsdp"),
        P(None, "fsdp", "mp"),
        P(None, "mp", "fsdp"),
    )
    return jax.shard_map(local, mesh=mesh, in_specs=in_specs, out_specs=out_specs, check_vma=False)
```
